32 devices in a mesh: grid: 16 (over z, x, core), orb: 2 (over y).
Axes of the slice: x: 2, y: 2, z: 4, core: 2. Of those that a mesh axis runs over, the one named last changes fastest.
Arguments:
- orbitals: bfloat16 [1024, 8, 64, 128], P('orb', None, 'grid'), may hold values from -0.0234375 to 0.0234375
- rotated_adj: bfloat16 [128, 8, 64, 128], P(None, None, 'grid'), may hold values from -6 to 6
- level_adj: float32 [128], replicated, may hold values from -240 to 240
- rotation: bfloat16 [1024, 1024], replicated, may hold values from -0.1875 to 0.1875
- gap_inverse: float32 [1024, 1024], P('orb'), may hold values from -10 to 10, as said below
- potential: float32 [8, 64, 128], P(None, 'grid'), may hold values from -4 to 2
- window_cols: int32 [128], replicated, may hold values from 0 to 1023, as said below
- tile_map: int32 [8], replicated, may hold values from 0 to 7, each once
Outputs:
- orbital_adj: bfloat16 [1024, 8, 64, 128], P('orb', None, 'grid')
The draws below stay inside these ranges and needn't reach their ends.
Inputs may be any that keep to these rules, and one draw needn't show every extreme that they name: `gap_inverse`: entry (i, j) is (l_j - l_i) / ((l_j - l_i) squared + 0.0025) for some real levels l, held within the range. `window_cols`: 128 distinct column indices, among them 0 and 1023. `tile_map`: each tile number once.
All inputs are finite; a program needn't handle non-finite values.
Results may differ from the reference program's by a relative error of at most 0.0069.
Values may be sent and summed in bfloat16 or wider, within the bound.
A program may use at most 192 MiB of HBM per device.

```python
import jax
import jax.numpy as jnp
from jax import lax

NORB = 1024
W = 128
TB = 128
NP = 8
NX = 128
NY = 64
NTILE = 8
NCELLS = 65536
N_ORB = 2


def draw_gap_inverse(key, part):
    key = jax.random.fold_in(key, 11)
    levels = jax.random.uniform(key, (NORB,), jnp.float32, -0.3, 0.3)
    spacing = levels[None, :] - levels[:, None]
    return jnp.clip(spacing / (spacing * spacing + 0.0025), -10.0, 10.0)


def draw_window_cols(key, part):
    key = jax.random.fold_in(key, 23)
    inner_key, order_key = jax.random.split(key)
    middle = jax.random.permutation(inner_key, NORB - 2)[:W - 2].astype(jnp.int32) + 1
    extremes = jnp.array([0, NORB - 1], dtype=jnp.int32)
    chosen = jnp.concatenate([extremes, middle])
    return jax.random.permutation(order_key, chosen).astype(jnp.int32)


def shard_levels(key, shape, cuts, low, high):
    def one(axis_at, parts):
        steps = jax.random.uniform(jax.random.fold_in(jax.random.fold_in(key, 6), axis_at), (parts,), jnp.float32, low / len(cuts), high / len(cuts))
        return jnp.repeat(jnp.exp(steps), shape[axis_at] // parts).reshape((-1,) + (1,) * (len(shape) - axis_at - 1))

    loudness = one(*cuts[0])
    for cut in cuts[1:]:
        loudness = loudness * one(*cut)
    return loudness


def bell_draw(stream_key, dims, scale, limit, cuts=(), kind=jnp.bfloat16):
    values = scale * jax.random.normal(stream_key, dims, jnp.float32)
    if cuts:
        values = values * shard_levels(stream_key, dims, cuts, -0.22, 0.18)
    return jnp.clip(values, -limit, limit).astype(kind)


def setup_inputs(seed: int = 0) -> dict:
    streams_of = jax.random.split(jax.random.key(seed), 9)
    orbitals = bell_draw(streams_of[0], (NORB, NP, NY, NX), NCELLS ** -0.5, 0.0234375, ((0, 2), (2, 16)))
    rotated_adj = bell_draw(streams_of[1], (W, NP, NY, NX), 1.0, 6.0, ((2, 16),))
    level_adj = bell_draw(streams_of[2], (W,), 40.0, 240.0, (), jnp.float32)
    rotation = bell_draw(streams_of[3], (NORB, NORB), NORB ** -0.5, 0.1875)
    gap_inverse = draw_gap_inverse(jax.random.fold_in(streams_of[8], 71), 0)
    potential = jnp.clip(-4.0 + 6.0 * jax.random.uniform(streams_of[5], (NP, NY, NX), jnp.float32) ** shard_levels(streams_of[5], (NP, NY, NX), ((1, 16),), -0.2, 0.2), -4.0, 2.0)
    window_cols = draw_window_cols(jax.random.fold_in(streams_of[8], 71), 0)
    tile_map = jax.random.permutation(streams_of[7], NTILE).astype(jnp.int32)
    return {"orbitals": orbitals, "rotated_adj": rotated_adj, "level_adj": level_adj, "rotation": rotation, "gap_inverse": gap_inverse, "potential": potential, "window_cols": window_cols, "tile_map": tile_map}


def second_diff(field, along):
    nearest = jnp.roll(field, 1, along) + jnp.roll(field, -1, along)
    farther = jnp.roll(field, 2, along) + jnp.roll(field, -2, along)
    return (16.0 * nearest - farther - 30.0 * field) / 12.0


def apply_block(fields, potential):
    field = fields.astype(jnp.float32)
    laplace = second_diff(field, 1) + second_diff(field, 2) + second_diff(field, 3)
    return (-0.5 * laplace + potential[None] * field).astype(jnp.bfloat16)


def reference(orbitals, rotated_adj, level_adj, rotation, gap_inverse, potential, window_cols, tile_map):
    cell_count = NP * NY * NX
    flat_orbs = orbitals.reshape(NORB, cell_count)
    flat_adj = rotated_adj.reshape(W, cell_count)
    cell_dims = (((1,), (1,)), ((), ()))
    orb_dims = (((0,), (0,)), ((), ()))
    correlation = lax.dot_general(flat_orbs, flat_adj, cell_dims, preferred_element_type=jnp.float32)
    offsets = jnp.arange(TB, dtype=jnp.int32)
    source_rows = (tile_map[:, None] * TB + offsets[None, :]).reshape(NORB)
    stored = jnp.take(rotation, source_rows, axis=0)
    stored_wide = stored.astype(jnp.float32)
    coupling_in = lax.dot_general(stored_wide, correlation, orb_dims, precision=lax.Precision.HIGHEST)
    gap_cols = jnp.take(gap_inverse, window_cols, axis=1)
    level_rows = jnp.arange(NORB, dtype=jnp.int32)
    diagonal = jnp.where(level_rows[:, None] == window_cols[None, :], level_adj[None, :], 0.0)
    coupling = gap_cols * coupling_in + diagonal
    left_factor = jnp.dot(stored_wide, coupling, precision=lax.Precision.HIGHEST).astype(jnp.bfloat16)
    right_factor = jnp.take(stored, window_cols, axis=1)
    factors = jnp.concatenate([left_factor, right_factor], axis=1)
    per_block = NORB // N_ORB
    summed = jnp.zeros((2 * W, cell_count), jnp.float32)
    for block_idx in range(N_ORB):
        lower = block_idx * per_block
        term = lax.dot_general(factors[lower:lower + per_block], flat_orbs[lower:lower + per_block], orb_dims, preferred_element_type=jnp.float32).astype(jnp.bfloat16)
        term = lax.optimization_barrier(term)
        summed = summed + term.astype(jnp.float32)
    combined = summed.astype(jnp.bfloat16).reshape(8, (2 * W) // 8, NP, NY, NX)
    applied = lax.map(lambda fields: apply_block(fields, potential), combined)
    stacked = jnp.concatenate([flat_adj, applied.reshape(2 * W, cell_count)], axis=0)
    mix_coeffs = jnp.concatenate([right_factor, right_factor, left_factor], axis=1)
    row_parts = mix_coeffs.reshape(8, NORB // 8, 3 * W)
    result = lax.map(lambda row_part: jnp.dot(row_part, stacked, preferred_element_type=jnp.float32).astype(jnp.bfloat16), row_parts)
    return result.reshape(NORB, NP, NY, NX)
```

```python
import functools

import jax
import jax.numpy as jnp
from jax import lax
from jax.experimental import pallas as pl
from jax.experimental.pallas import tpu as pltpu
from jax.sharding import PartitionSpec as P

MESH = pl.DeviceIdType.MESH
NCH = 4
F32 = jnp.float32
BF16 = jnp.bfloat16
NT = (((1,), (1,)), ((), ()))
NN = (((1,), (0,)), ((), ()))


def dot(a, b, dims):
    return lax.dot_general(a, b, dims, preferred_element_type=F32)


def split3(x):
    hi = x.astype(BF16)
    rest = x - hi.astype(F32)
    mid = rest.astype(BF16)
    low = (rest - mid.astype(F32)).astype(BF16)
    return hi, mid, low


def fields_kernel(
    n, planes, rows,
    orb_ref, adj_ref, stored_ref, gap_ref, level_ref, cols_ref, pot_ref,
    app_ref, fac_ref,
    corr, rs_buf, ag_buf, gap_all, part, peer, wide,
    rs_send, rs_recv, ag_send, ag_recv, gap_send, gap_recv,
    sum_send, sum_recv, up_send, up_recv, down_send, down_recv,
):
    slabs, local_orbs, nx = orb_ref.shape
    w = adj_ref.shape[1]
    norb = stored_ref.shape[0]
    chunk = local_orbs // n
    wc = w // NCH
    total = 2 * n
    g = lax.axis_index("grid")
    o = lax.axis_index("orb")
    me = o * n + g
    other = 1 - o
    after = lax.rem(g + 1, n)
    before = lax.rem(g + n - 1, n)

    barrier = pltpu.get_barrier_semaphore()

    def greet(k, _):
        to = lax.rem(me + k, total)
        pl.semaphore_signal(
            barrier, inc=1, device_id=(lax.rem(to, n), to // n), device_id_type=MESH
        )
        return 0

    lax.fori_loop(1, total, greet, 0)

    corr[...] = jnp.zeros_like(corr)

    def corr_step(r, _):
        corr[...] += dot(orb_ref[r], adj_ref[r], NT).reshape(corr.shape)
        return 0

    lax.fori_loop(0, slabs, corr_step, 0)
    pl.semaphore_wait(barrier, total - 1)

    def rs_copy(k):
        to = lax.rem(g + k, n)
        return pltpu.make_async_remote_copy(
            src_ref=corr.at[to], dst_ref=rs_buf.at[k],
            send_sem=rs_send.at[k], recv_sem=rs_recv.at[k],
            device_id=(to, o), device_id_type=MESH,
        )

    def rs_start(k, _):
        rs_copy(k).start()
        return 0

    lax.fori_loop(1, n, rs_start, 0)

    def sum_copy(half, ch):
        i = half * NCH + ch
        return pltpu.make_async_remote_copy(
            src_ref=part.at[i], dst_ref=peer.at[i],
            send_sem=sum_send.at[i], recv_sem=sum_recv.at[i],
            device_id=(g, other), device_id_type=MESH,
        )

    def up_copy(half, ch):
        i = half * NCH + ch
        return pltpu.make_async_remote_copy(
            src_ref=wide.at[i, pl.ds(rows, 2)], dst_ref=wide.at[i, pl.ds(0, 2)],
            send_sem=up_send.at[i], recv_sem=up_recv.at[i],
            device_id=(after, o), device_id_type=MESH,
        )

    def down_copy(half, ch):
        i = half * NCH + ch
        return pltpu.make_async_remote_copy(
            src_ref=wide.at[i, pl.ds(2, 2)], dst_ref=wide.at[i, pl.ds(rows + 2, 2)],
            send_sem=down_send.at[i], recv_sem=down_recv.at[i],
            device_id=(before, o), device_id_type=MESH,
        )

    def send_partials(half, factor_t):
        def step(r, _):
            term = dot(factor_t, orb_ref[r], NN).astype(BF16)
            for ch in range(NCH):
                part[half * NCH + ch, r] = term[ch * wc : (ch + 1) * wc]
            return 0

        lax.fori_loop(0, slabs, step, 0)
        for ch in range(NCH):
            sum_copy(half, ch).start()

    mine = pl.ds(pl.multiple_of(o * local_orbs, local_orbs), local_orbs)
    level_rows = lax.broadcasted_iota(jnp.int32, (w, norb), 1)
    hot = level_rows == cols_ref[...]
    hot16 = hot.astype(F32).astype(BF16)
    right_t = dot(hot16, stored_ref[mine, :], NT).astype(BF16)
    fac_ref[0] = right_t
    send_partials(0, right_t)

    hi, mid, low = split3(gap_ref[...])
    gap_all[o] = dot(hot16, hi, NT) + dot(hot16, mid, NT) + dot(hot16, low, NT)
    gap_copy = pltpu.make_async_remote_copy(
        src_ref=gap_all.at[o], dst_ref=gap_all.at[o],
        send_sem=gap_send, recv_sem=gap_recv,
        device_id=(g, other), device_id_type=MESH,
    )
    gap_copy.start()

    ag_buf[me] = corr[g]

    def rs_take(k, _):
        rs_copy(k).wait_recv()
        ag_buf[me] += rs_buf[k]
        return 0

    lax.fori_loop(1, n, rs_take, 0)

    def ag_copy(k):
        to = lax.rem(me + k, total)
        return pltpu.make_async_remote_copy(
            src_ref=ag_buf.at[me], dst_ref=ag_buf.at[me],
            send_sem=ag_send.at[k], recv_sem=ag_recv.at[k],
            device_id=(lax.rem(to, n), to // n), device_id_type=MESH,
        )

    def ag_start(k, _):
        ag_copy(k).start()
        return 0

    def ag_take(k, _):
        ag_copy(k).wait_recv()
        return 0

    lax.fori_loop(1, total, ag_start, 0)
    lax.fori_loop(1, total, ag_take, 0)
    gap_copy.wait_recv()

    corr_t = ag_buf[...].reshape(norb, w).T
    parts_t = jnp.concatenate(split3(corr_t), axis=0)
    rotated = dot(parts_t, stored_ref[...], NN)
    coupling_in = rotated[:w] + rotated[w : 2 * w] + rotated[2 * w :]
    gap_cols = jnp.concatenate([gap_all[0], gap_all[1]], axis=1)
    coupling = gap_cols * coupling_in + jnp.where(hot, level_ref[...], 0.0)
    mixed = dot(jnp.concatenate(split3(coupling), axis=0), stored_ref[mine, :], NT)
    left_t = (mixed[:w] + mixed[w : 2 * w] + mixed[2 * w :]).astype(BF16)
    fac_ref[1] = left_t
    send_partials(1, left_t)

    def combine(half, ch):
        i = half * NCH + ch
        sum_copy(half, ch).wait_recv()

        def step(p, _):
            for y in range(rows):
                r = p * rows + y
                wide[i, 2 + y, p] = (
                    part[i, r].astype(F32) + peer[i, r].astype(F32)
                ).astype(BF16)
            return 0

        lax.fori_loop(0, planes, step, 0)
        up_copy(half, ch).start()
        down_copy(half, ch).start()

    def stencil(half, ch):
        i = half * NCH + ch
        up_copy(half, ch).wait_recv()
        down_copy(half, ch).wait_recv()

        def step(p, _):
            lines = [wide[i, y, p].astype(F32) for y in range(rows + 4)]
            near_planes = [lax.rem(p + d, planes) for d in (1, planes - 1)]
            far_planes = [lax.rem(p + d, planes) for d in (2, planes - 2)]
            for y in range(rows):
                f = lines[y + 2]
                near = lines[y + 1] + lines[y + 3]
                far = lines[y] + lines[y + 4]
                for q in near_planes:
                    near = near + wide[i, 2 + y, q].astype(F32)
                for q in far_planes:
                    far = far + wide[i, 2 + y, q].astype(F32)
                near = near + pltpu.roll(f, 1, 1) + pltpu.roll(f, nx - 1, 1)
                far = far + pltpu.roll(f, 2, 1) + pltpu.roll(f, nx - 2, 1)
                r = p * rows + y
                diag = 3.75 + pot_ref[pl.ds(r, 1), :]
                value = diag * f - (2.0 / 3.0) * near + (1.0 / 24.0) * far
                app_ref[r, half * w + ch * wc : half * w + (ch + 1) * wc] = value.astype(BF16)
            return 0

        lax.fori_loop(0, planes, step, 0)

    for half in range(2):
        for ch in range(NCH):
            combine(half, ch)
            if ch:
                stencil(half, ch - 1)
        stencil(half, NCH - 1)

    def rs_done(k, _):
        rs_copy(k).wait_send()
        return 0

    def ag_done(k, _):
        ag_copy(k).wait_send()
        return 0

    lax.fori_loop(1, n, rs_done, 0)
    lax.fori_loop(1, total, ag_done, 0)
    gap_copy.wait_send()
    for half in range(2):
        for ch in range(NCH):
            sum_copy(half, ch).wait_send()
            up_copy(half, ch).wait_send()
            down_copy(half, ch).wait_send()


def local(
    orbitals, rotated_adj, level_adj, rotation, gap_inverse, potential, window_cols, tile_map
):
    local_orbs, planes, rows, nx = orbitals.shape
    w = rotated_adj.shape[0]
    norb = rotation.shape[0]
    tiles = tile_map.shape[0]
    n = lax.axis_size("grid")
    slabs = planes * rows
    chunk = local_orbs // n
    wc = w // NCH
    orb_r = orbitals.reshape(local_orbs, slabs, nx).transpose(1, 0, 2)
    adj_r = rotated_adj.reshape(w, slabs, nx).transpose(1, 0, 2)
    stored = jnp.take(
        rotation.reshape(tiles, norb // tiles, norb), tile_map, axis=0, mode="clip"
    ).reshape(norb, norb)
    vmem = pl.BlockSpec(memory_space=pltpu.VMEM)
    dma = pltpu.SemaphoreType.DMA
    applied, factors = pl.pallas_call(
        functools.partial(fields_kernel, n, planes, rows),
        out_shape=(
            jax.ShapeDtypeStruct((slabs, 2 * w, nx), BF16),
            jax.ShapeDtypeStruct((2, w, local_orbs), BF16),
        ),
        in_specs=[vmem] * 7,
        out_specs=(vmem, vmem),
        scratch_shapes=[
            pltpu.VMEM((n, chunk, w), F32),
            pltpu.VMEM((n, chunk, w), F32),
            pltpu.VMEM((2 * n, chunk, w), F32),
            pltpu.VMEM((2, w, local_orbs), F32),
            pltpu.VMEM((2 * NCH, slabs, wc, nx), BF16),
            pltpu.VMEM((2 * NCH, slabs, wc, nx), BF16),
            pltpu.VMEM((2 * NCH, rows + 4, planes, wc, nx), BF16),
            dma((n,)), dma((n,)), dma((2 * n,)), dma((2 * n,)), dma, dma,
            dma((2 * NCH,)), dma((2 * NCH,)), dma((2 * NCH,)),
            dma((2 * NCH,)), dma((2 * NCH,)), dma((2 * NCH,)),
        ],
        compiler_params=pltpu.CompilerParams(
            collective_id=0, has_side_effects=True, vmem_limit_bytes=56 * 1024 * 1024
        ),
    )(
        orb_r, adj_r, stored, gap_inverse, level_adj.reshape(w, 1),
        window_cols.reshape(w, 1), potential.reshape(slabs, nx),
    )
    stacked = jnp.concatenate([adj_r, applied], axis=1)
    mix_t = jnp.concatenate([factors[0], factors[1], factors[0]], axis=0)
    result = lax.dot_general(
        mix_t, stacked, (((0,), (1,)), ((), ())), preferred_element_type=F32
    ).astype(BF16)
    return result.reshape(orbitals.shape)


def solution(mesh):
    in_specs = (
        P("orb", None, "grid", None),
        P(None, None, "grid", None),
        P(),
        P(),
        P("orb", None),
        P(None, "grid", None),
        P(),
        P(),
    )
    out_specs = P("orb", None, "grid", None)
    return jax.shard_map(local, mesh=mesh, in_specs=in_specs, out_specs=out_specs, check_vma=False)
```

```python
import functools

import jax
import jax.numpy as jnp
from jax import lax
from jax.experimental import pallas as pl
from jax.experimental.pallas import tpu as pltpu
from jax.sharding import PartitionSpec as P

MESH = pl.DeviceIdType.MESH
NCH = 8
EARLY = 2
F32 = jnp.float32
BF16 = jnp.bfloat16
NT = (((1,), (1,)), ((), ()))
NN = (((1,), (0,)), ((), ()))


def dot(a, b, dims):
    return lax.dot_general(a, b, dims, preferred_element_type=F32)


def split3(x):
    hi = x.astype(BF16)
    rest = x - hi.astype(F32)
    mid = rest.astype(BF16)
    low = (rest - mid.astype(F32)).astype(BF16)
    return hi, mid, low


def fields_kernel(
    n, planes, rows,
    orb_ref, adj_ref, stored_ref, gap_ref, level_ref, cols_ref, pot_ref,
    app_ref, fac_ref,
    corr, rs_buf, ag_buf, gap_all, part, peer, wide,
    rs_send, rs_recv, ag_send, ag_recv, gap_send, gap_recv,
    sum_send, sum_recv, up_send, up_recv, down_send, down_recv,
):
    slabs, local_orbs, nx = orb_ref.shape
    w = adj_ref.shape[1]
    norb = stored_ref.shape[0]
    wc = w // NCH
    g = lax.axis_index("grid")
    o = lax.axis_index("orb")
    me = o * n + g
    other = 1 - o
    after = lax.rem(g + 1, n)
    before = lax.rem(g + n - 1, n)

    barrier = pltpu.get_barrier_semaphore()

    def greet(k, _):
        pl.semaphore_signal(
            barrier, inc=1, device_id=(lax.rem(g + k, n), o), device_id_type=MESH
        )
        return 0

    pl.semaphore_signal(barrier, inc=1, device_id=(g, other), device_id_type=MESH)
    lax.fori_loop(1, n, greet, 0)

    def rs_copy(k):
        to = lax.rem(g + k, n)
        return pltpu.make_async_remote_copy(
            src_ref=corr.at[to], dst_ref=rs_buf.at[k],
            send_sem=rs_send.at[k], recv_sem=rs_recv.at[k],
            device_id=(to, o), device_id_type=MESH,
        )

    def rs_start(k, _):
        rs_copy(k).start()
        return 0

    def sum_copy(half, ch):
        i = half * NCH + ch
        return pltpu.make_async_remote_copy(
            src_ref=part.at[i], dst_ref=peer.at[i],
            send_sem=sum_send.at[i], recv_sem=sum_recv.at[i],
            device_id=(g, other), device_id_type=MESH,
        )

    def up_copy(half, ch):
        i = half * NCH + ch
        return pltpu.make_async_remote_copy(
            src_ref=wide.at[i, pl.ds(rows, 2)], dst_ref=wide.at[i, pl.ds(0, 2)],
            send_sem=up_send.at[i], recv_sem=up_recv.at[i],
            device_id=(after, o), device_id_type=MESH,
        )

    def down_copy(half, ch):
        i = half * NCH + ch
        return pltpu.make_async_remote_copy(
            src_ref=wide.at[i, pl.ds(2, 2)], dst_ref=wide.at[i, pl.ds(rows + 2, 2)],
            send_sem=down_send.at[i], recv_sem=down_recv.at[i],
            device_id=(before, o), device_id_type=MESH,
        )

    def partials(half, factor_t):
        def step(k, _):
            pair = jnp.concatenate([orb_ref[2 * k], orb_ref[2 * k + 1]], axis=1)
            term = dot(factor_t, pair, NN).astype(BF16)
            for ch in range(NCH):
                fields = term[ch * wc : (ch + 1) * wc]
                part[half * NCH + ch, 2 * k] = fields[:, :nx]
                part[half * NCH + ch, 2 * k + 1] = fields[:, nx:]
            return 0

        lax.fori_loop(0, slabs // 2, step, 0)

    def column(row_ref):
        row = row_ref[...].astype(F32)
        return jnp.broadcast_to(row, (w, w)).T[:, :1]

    mine = pl.ds(pl.multiple_of(o * local_orbs, local_orbs), local_orbs)
    level_rows = lax.broadcasted_iota(jnp.int32, (w, norb), 1).astype(F32)
    hot = level_rows == column(cols_ref)
    hot16 = hot.astype(F32).astype(BF16)
    right_t = dot(hot16, stored_ref[mine, :], NT).astype(BF16)
    fac_ref[0] = right_t
    fac_ref[2] = right_t

    hi, mid, low = split3(gap_ref[...])
    gap_all[o] = dot(hot16, hi, NT) + dot(hot16, mid, NT) + dot(hot16, low, NT)
    gap_copy = pltpu.make_async_remote_copy(
        src_ref=gap_all.at[o], dst_ref=gap_all.at[o],
        send_sem=gap_send, recv_sem=gap_recv,
        device_id=(g, other), device_id_type=MESH,
    )
    pl.semaphore_wait(barrier, n)
    gap_copy.start()
    partials(0, right_t)
    for ch in range(EARLY):
        sum_copy(0, ch).start()

    corr[...] = jnp.zeros_like(corr)

    def corr_step(k, _):
        orbs = jnp.concatenate([orb_ref[4 * k + i] for i in range(4)], axis=1)
        adjs = jnp.concatenate([adj_ref[4 * k + i] for i in range(4)], axis=1)
        corr[...] += dot(orbs, adjs, NT).reshape(corr.shape)
        return 0

    lax.fori_loop(0, slabs // 4, corr_step, 0)
    lax.fori_loop(1, n, rs_start, 0)

    def stack_step(r, _):
        app_ref[r, :w] = adj_ref[r]
        return 0

    lax.fori_loop(0, slabs, stack_step, 0)

    ag_buf[me] = corr[g]

    def rs_take(k, _):
        rs_copy(k).wait_recv()
        ag_buf[me] += rs_buf[k]
        return 0

    lax.fori_loop(1, n, rs_take, 0)

    theirs = other * n + g
    cross_copy = pltpu.make_async_remote_copy(
        src_ref=ag_buf.at[me], dst_ref=ag_buf.at[me],
        send_sem=ag_send.at[0], recv_sem=ag_recv.at[0],
        device_id=(g, other), device_id_type=MESH,
    )

    def ag_copy(k, slot, first):
        return pltpu.make_async_remote_copy(
            src_ref=ag_buf.at[slot], dst_ref=ag_buf.at[slot],
            send_sem=ag_send.at[first + k], recv_sem=ag_recv.at[first + k],
            device_id=(lax.rem(g + k, n), o), device_id_type=MESH,
        )

    def ag_start(k, _):
        ag_copy(k, me, 0).start()
        return 0

    def ag_forward(k, _):
        ag_copy(k, theirs, n).start()
        return 0

    def ag_take(k, _):
        ag_copy(k, me, 0).wait_recv()
        ag_copy(k, theirs, n).wait_recv()
        return 0

    cross_copy.start()
    lax.fori_loop(1, n, ag_start, 0)
    for ch in range(EARLY, NCH):
        sum_copy(0, ch).start()
    cross_copy.wait_recv()
    lax.fori_loop(1, n, ag_forward, 0)
    lax.fori_loop(1, n, ag_take, 0)
    gap_copy.wait_recv()

    corr_t = ag_buf[...].reshape(norb, w).T
    parts_t = jnp.concatenate(split3(corr_t), axis=0)
    rotated = dot(parts_t, stored_ref[...], NN)
    coupling_in = rotated[:w] + rotated[w : 2 * w] + rotated[2 * w :]
    gap_cols = jnp.concatenate([gap_all[0], gap_all[1]], axis=1)
    coupling = gap_cols * coupling_in + jnp.where(hot, column(level_ref), 0.0)
    mixed = dot(jnp.concatenate(split3(coupling), axis=0), stored_ref[mine, :], NT)
    left_t = (mixed[:w] + mixed[w : 2 * w] + mixed[2 * w :]).astype(BF16)
    fac_ref[1] = left_t
    partials(1, left_t)
    for ch in range(NCH):
        sum_copy(1, ch).start()

    def combine(half, ch):
        i = half * NCH + ch
        sum_copy(half, ch).wait_recv()

        def step(p, _):
            for y in range(rows):
                r = p * rows + y
                wide[i, 2 + y, p] = (
                    part[i, r].astype(F32) + peer[i, r].astype(F32)
                ).astype(BF16)
            return 0

        lax.fori_loop(0, planes, step, 0)
        up_copy(half, ch).start()
        down_copy(half, ch).start()

    def stencil(half, ch):
        i = half * NCH + ch
        up_copy(half, ch).wait_recv()
        down_copy(half, ch).wait_recv()
        first = (half + 1) * w + ch * wc

        def step(p, _):
            lines = [wide[i, y, p].astype(F32) for y in range(rows + 4)]
            near_planes = [lax.rem(p + d, planes) for d in (1, planes - 1)]
            far_planes = [lax.rem(p + d, planes) for d in (2, planes - 2)]
            for y in range(rows):
                f = lines[y + 2]
                near = lines[y + 1] + lines[y + 3]
                far = lines[y] + lines[y + 4]
                for q in near_planes:
                    near = near + wide[i, 2 + y, q].astype(F32)
                for q in far_planes:
                    far = far + wide[i, 2 + y, q].astype(F32)
                near = near + pltpu.roll(f, 1, 1) + pltpu.roll(f, nx - 1, 1)
                far = far + pltpu.roll(f, 2, 1) + pltpu.roll(f, nx - 2, 1)
                r = p * rows + y
                diag = 3.75 + pot_ref[pl.ds(r, 1), :]
                value = diag * f - (2.0 / 3.0) * near + (1.0 / 24.0) * far
                app_ref[r, first : first + wc] = value.astype(BF16)
            return 0

        lax.fori_loop(0, planes, step, 0)

    for half in range(2):
        for ch in range(NCH):
            combine(half, ch)
            if ch:
                stencil(half, ch - 1)
        stencil(half, NCH - 1)

    def rs_done(k, _):
        rs_copy(k).wait_send()
        return 0

    def ag_done(k, _):
        ag_copy(k, me, 0).wait_send()
        ag_copy(k, theirs, n).wait_send()
        return 0

    lax.fori_loop(1, n, rs_done, 0)
    lax.fori_loop(1, n, ag_done, 0)
    cross_copy.wait_send()
    gap_copy.wait_send()
    for half in range(2):
        for ch in range(NCH):
            sum_copy(half, ch).wait_send()
            up_copy(half, ch).wait_send()
            down_copy(half, ch).wait_send()


def local(
    orbitals, rotated_adj, level_adj, rotation, gap_inverse, potential, window_cols, tile_map
):
    local_orbs, planes, rows, nx = orbitals.shape
    w = rotated_adj.shape[0]
    norb = rotation.shape[0]
    n = lax.axis_size("grid")
    slabs = planes * rows
    chunk = local_orbs // n
    wc = w // NCH
    orb_r = orbitals.reshape(local_orbs, slabs, nx).transpose(1, 0, 2)
    adj_r = rotated_adj.reshape(w, slabs, nx).transpose(1, 0, 2)
    tiles = tile_map.shape[0]
    stored = jnp.take(
        rotation.reshape(tiles, norb // tiles, norb), tile_map, axis=0, mode="clip"
    ).reshape(norb, norb)
    vmem = pl.BlockSpec(memory_space=pltpu.VMEM)
    dma = pltpu.SemaphoreType.DMA
    stacked, factors = pl.pallas_call(
        functools.partial(fields_kernel, n, planes, rows),
        out_shape=(
            jax.ShapeDtypeStruct((slabs, 3 * w, nx), BF16),
            jax.ShapeDtypeStruct((3, w, local_orbs), BF16),
        ),
        in_specs=[vmem] * 7,
        out_specs=(vmem, vmem),
        scratch_shapes=[
            pltpu.VMEM((n, chunk, w), F32),
            pltpu.VMEM((n, chunk, w), F32),
            pltpu.VMEM((2 * n, chunk, w), F32),
            pltpu.VMEM((2, w, local_orbs), F32),
            pltpu.VMEM((2 * NCH, slabs, wc, nx), BF16),
            pltpu.VMEM((2 * NCH, slabs, wc, nx), BF16),
            pltpu.VMEM((2 * NCH, rows + 4, planes, wc, nx), BF16),
            dma((n,)), dma((n,)), dma((2 * n,)), dma((2 * n,)), dma, dma,
            dma((2 * NCH,)), dma((2 * NCH,)), dma((2 * NCH,)),
            dma((2 * NCH,)), dma((2 * NCH,)), dma((2 * NCH,)),
        ],
        compiler_params=pltpu.CompilerParams(
            collective_id=0, has_side_effects=True, vmem_limit_bytes=56 * 1024 * 1024
        ),
    )(
        orb_r, adj_r, stored, gap_inverse, level_adj.reshape(1, w),
        window_cols.reshape(1, w), potential.reshape(slabs, nx),
    )
    mix_t = factors.reshape(3 * w, local_orbs)
    result = lax.dot_general(
        mix_t, stacked, (((0,), (1,)), ((), ())), preferred_element_type=F32
    ).astype(BF16)
    return result.reshape(orbitals.shape)


def solution(mesh):
    in_specs = (
        P("orb", None, "grid", None),
        P(None, None, "grid", None),
        P(),
        P(),
        P("orb", None),
        P(None, "grid", None),
        P(),
        P(),
    )
    out_specs = P("orb", None, "grid", None)
    return jax.shard_map(local, mesh=mesh, in_specs=in_specs, out_specs=out_specs, check_vma=False)
```

```python
import functools

import jax
import jax.numpy as jnp
from jax import lax
from jax.experimental import pallas as pl
from jax.experimental.pallas import tpu as pltpu
from jax.sharding import PartitionSpec as P

MESH = pl.DeviceIdType.MESH
NCH = 8
EARLY = 2
F32 = jnp.float32
BF16 = jnp.bfloat16
NT = (((1,), (1,)), ((), ()))
NN = (((1,), (0,)), ((), ()))


def dot(a, b, dims):
    return lax.dot_general(a, b, dims, preferred_element_type=F32)


def split3(x):
    hi = x.astype(BF16)
    rest = x - hi.astype(F32)
    mid = rest.astype(BF16)
    low = (rest - mid.astype(F32)).astype(BF16)
    return hi, mid, low


def fields_kernel(
    n, planes, rows,
    orb_ref, adj_ref, stored_ref, gap_ref, level_ref, cols_ref, pot_ref,
    out_ref,
    app_ref, mix_ref, mixed_rows, corr, rs_buf, ag_buf, gap_all, part, peer, wide,
    rs_send, rs_recv, ag_send, ag_recv, gap_send, gap_recv,
    sum_send, sum_recv, up_send, up_recv, down_send, down_recv,
):
    slabs, local_orbs, nx = orb_ref.shape
    w = adj_ref.shape[1]
    norb = stored_ref.shape[0]
    wc = w // NCH
    g = lax.axis_index("grid")
    o = lax.axis_index("orb")
    me = o * n + g
    other = 1 - o
    after = lax.rem(g + 1, n)
    before = lax.rem(g + n - 1, n)

    barrier = pltpu.get_barrier_semaphore()

    def greet(k, _):
        pl.semaphore_signal(
            barrier, inc=1, device_id=(lax.rem(g + k, n), o), device_id_type=MESH
        )
        return 0

    pl.semaphore_signal(barrier, inc=1, device_id=(g, other), device_id_type=MESH)
    lax.fori_loop(1, n, greet, 0)

    def rs_copy(k):
        to = lax.rem(g + k, n)
        return pltpu.make_async_remote_copy(
            src_ref=corr.at[to], dst_ref=rs_buf.at[k],
            send_sem=rs_send.at[k], recv_sem=rs_recv.at[k],
            device_id=(to, o), device_id_type=MESH,
        )

    def rs_start(k, _):
        rs_copy(k).start()
        return 0

    def sum_copy(half, ch):
        i = half * NCH + ch
        return pltpu.make_async_remote_copy(
            src_ref=part.at[i], dst_ref=peer.at[i],
            send_sem=sum_send.at[i], recv_sem=sum_recv.at[i],
            device_id=(g, other), device_id_type=MESH,
        )

    def up_copy(half, ch):
        i = half * NCH + ch
        return pltpu.make_async_remote_copy(
            src_ref=wide.at[i, pl.ds(rows, 2)], dst_ref=wide.at[i, pl.ds(0, 2)],
            send_sem=up_send.at[i], recv_sem=up_recv.at[i],
            device_id=(after, o), device_id_type=MESH,
        )

    def down_copy(half, ch):
        i = half * NCH + ch
        return pltpu.make_async_remote_copy(
            src_ref=wide.at[i, pl.ds(2, 2)], dst_ref=wide.at[i, pl.ds(rows + 2, 2)],
            send_sem=down_send.at[i], recv_sem=down_recv.at[i],
            device_id=(before, o), device_id_type=MESH,
        )

    def partials(half, factor_t):
        def step(k, _):
            pair = jnp.concatenate([orb_ref[2 * k], orb_ref[2 * k + 1]], axis=1)
            term = dot(factor_t, pair, NN).astype(BF16)
            for ch in range(NCH):
                fields = term[ch * wc : (ch + 1) * wc]
                part[half * NCH + ch, 2 * k] = fields[:, :nx]
                part[half * NCH + ch, 2 * k + 1] = fields[:, nx:]
            return 0

        lax.fori_loop(0, slabs // 2, step, 0)

    def column(row_ref):
        row = row_ref[...].astype(F32)
        return jnp.broadcast_to(row, (w, w)).T[:, :1]

    mine = pl.ds(pl.multiple_of(o * local_orbs, local_orbs), local_orbs)
    level_rows = lax.broadcasted_iota(jnp.int32, (w, norb), 1).astype(F32)
    hot = level_rows == column(cols_ref)
    hot16 = hot.astype(F32).astype(BF16)
    right_t = dot(hot16, stored_ref[mine, :], NT).astype(BF16)
    mix_ref[:, :w] = right_t.astype(F32).T.astype(BF16)
    mix_ref[:, 2 * w :] = mix_ref[:, :w]

    hi, mid, low = split3(gap_ref[...])
    mine_gap = dot(hot16, hi, NT) + dot(hot16, mid, NT) + dot(hot16, low, NT)
    gap_all[o] = mine_gap.reshape(n, w // n, local_orbs)
    gap_cross = pltpu.make_async_remote_copy(
        src_ref=gap_all.at[o, g], dst_ref=gap_all.at[o, g],
        send_sem=gap_send.at[0], recv_sem=gap_recv.at[0],
        device_id=(g, other), device_id_type=MESH,
    )

    def gap_copy(k):
        return pltpu.make_async_remote_copy(
            src_ref=gap_all.at[other, g], dst_ref=gap_all.at[other, g],
            send_sem=gap_send.at[k], recv_sem=gap_recv.at[k],
            device_id=(lax.rem(g + k, n), o), device_id_type=MESH,
        )

    def gap_start(k, _):
        gap_copy(k).start()
        return 0

    pl.semaphore_wait(barrier, n)
    gap_cross.start()
    partials(0, right_t)
    for ch in range(EARLY):
        sum_copy(0, ch).start()
    gap_cross.wait_recv()
    lax.fori_loop(1, n, gap_start, 0)

    corr[...] = jnp.zeros_like(corr)

    def corr_step(k, _):
        orbs = jnp.concatenate([orb_ref[4 * k + i] for i in range(4)], axis=1)
        adjs = jnp.concatenate([adj_ref[4 * k + i] for i in range(4)], axis=1)
        corr[...] += dot(orbs, adjs, NT).reshape(corr.shape)
        return 0

    lax.fori_loop(0, slabs // 4, corr_step, 0)
    lax.fori_loop(1, n, rs_start, 0)

    def stack_step(r, _):
        app_ref[r, :w] = adj_ref[r]
        return 0

    lax.fori_loop(0, slabs, stack_step, 0)

    ag_buf[me] = corr[g]

    def rs_take(k, _):
        rs_copy(k).wait_recv()
        ag_buf[me] += rs_buf[k]
        return 0

    lax.fori_loop(1, n, rs_take, 0)

    theirs = other * n + g
    cross_copy = pltpu.make_async_remote_copy(
        src_ref=ag_buf.at[me], dst_ref=ag_buf.at[me],
        send_sem=ag_send.at[0], recv_sem=ag_recv.at[0],
        device_id=(g, other), device_id_type=MESH,
    )

    def ag_copy(k, slot, first):
        return pltpu.make_async_remote_copy(
            src_ref=ag_buf.at[slot], dst_ref=ag_buf.at[slot],
            send_sem=ag_send.at[first + k], recv_sem=ag_recv.at[first + k],
            device_id=(lax.rem(g + k, n), o), device_id_type=MESH,
        )

    def ag_start(k, _):
        ag_copy(k, me, 0).start()
        return 0

    def ag_forward(k, _):
        ag_copy(k, theirs, n).start()
        return 0

    def ag_take(k, _):
        ag_copy(k, me, 0).wait_recv()
        ag_copy(k, theirs, n).wait_recv()
        gap_copy(k).wait_recv()
        return 0

    cross_copy.start()
    lax.fori_loop(1, n, ag_start, 0)
    for ch in range(EARLY, NCH):
        sum_copy(0, ch).start()
    cross_copy.wait_recv()
    lax.fori_loop(1, n, ag_forward, 0)
    lax.fori_loop(1, n, ag_take, 0)

    corr_t = ag_buf[...].reshape(norb, w).T
    parts_t = jnp.concatenate(split3(corr_t), axis=0)
    rotated = dot(parts_t, stored_ref[...], NN)
    coupling_in = rotated[:w] + rotated[w : 2 * w] + rotated[2 * w :]
    gap_cols = jnp.concatenate([gap_all[i].reshape(w, local_orbs) for i in range(2)], axis=1)
    coupling = gap_cols * coupling_in + jnp.where(hot, column(level_ref), 0.0)
    mixed = dot(jnp.concatenate(split3(coupling), axis=0), stored_ref[mine, :], NT)
    left_t = (mixed[:w] + mixed[w : 2 * w] + mixed[2 * w :]).astype(BF16)
    partials(1, left_t)
    for ch in range(NCH):
        sum_copy(1, ch).start()
    mix_ref[:, w : 2 * w] = left_t.astype(F32).T.astype(BF16)

    def combine(half, ch):
        i = half * NCH + ch
        sum_copy(half, ch).wait_recv()

        def step(p, _):
            for y in range(rows):
                r = p * rows + y
                wide[i, 2 + y, p] = (
                    part[i, r].astype(F32) + peer[i, r].astype(F32)
                ).astype(BF16)
            return 0

        lax.fori_loop(0, planes, step, 0)
        up_copy(half, ch).start()
        down_copy(half, ch).start()

    def stencil(half, ch):
        i = half * NCH + ch
        up_copy(half, ch).wait_recv()
        down_copy(half, ch).wait_recv()
        first = (half + 1) * w + ch * wc

        def step(p, _):
            lines = [wide[i, y, p].astype(F32) for y in range(rows + 4)]
            near_planes = [lax.rem(p + d, planes) for d in (1, planes - 1)]
            far_planes = [lax.rem(p + d, planes) for d in (2, planes - 2)]
            for y in range(rows):
                f = lines[y + 2]
                near = lines[y + 1] + lines[y + 3]
                far = lines[y] + lines[y + 4]
                for q in near_planes:
                    near = near + wide[i, 2 + y, q].astype(F32)
                for q in far_planes:
                    far = far + wide[i, 2 + y, q].astype(F32)
                near = near + pltpu.roll(f, 1, 1) + pltpu.roll(f, nx - 1, 1)
                far = far + pltpu.roll(f, 2, 1) + pltpu.roll(f, nx - 2, 1)
                r = p * rows + y
                diag = 3.75 + pot_ref[pl.ds(r, 1), :]
                value = diag * f - (2.0 / 3.0) * near + (1.0 / 24.0) * far
                app_ref[r, first : first + wc] = value.astype(BF16)
            return 0

        lax.fori_loop(0, planes, step, 0)

    def pair_of(k, fields):
        return jnp.concatenate([app_ref[2 * k, fields], app_ref[2 * k + 1, fields]], axis=1)

    def mix_first(k, _):
        mixed_rows[k] = dot(mix_ref[:, : 2 * w], pair_of(k, slice(0, 2 * w)), NN)
        return 0

    def mix_last(k, _):
        rest = dot(mix_ref[:, 2 * w :], pair_of(k, slice(2 * w, 3 * w)), NN)
        value = (mixed_rows[k] + rest).astype(BF16)
        out_ref[2 * k] = value[:, :nx]
        out_ref[2 * k + 1] = value[:, nx:]
        return 0

    for half in range(2):
        for ch in range(NCH):
            combine(half, ch)
            if ch:
                stencil(half, ch - 1)
        stencil(half, NCH - 1)
        lax.fori_loop(0, slabs // 2, (mix_first, mix_last)[half], 0)

    def rs_done(k, _):
        rs_copy(k).wait_send()
        return 0

    def ag_done(k, _):
        ag_copy(k, me, 0).wait_send()
        ag_copy(k, theirs, n).wait_send()
        gap_copy(k).wait_send()
        return 0

    lax.fori_loop(1, n, rs_done, 0)
    lax.fori_loop(1, n, ag_done, 0)
    cross_copy.wait_send()
    gap_cross.wait_send()
    for half in range(2):
        for ch in range(NCH):
            sum_copy(half, ch).wait_send()
            up_copy(half, ch).wait_send()
            down_copy(half, ch).wait_send()


def local(
    orbitals, rotated_adj, level_adj, rotation, gap_inverse, potential, window_cols, tile_map
):
    local_orbs, planes, rows, nx = orbitals.shape
    w = rotated_adj.shape[0]
    norb = rotation.shape[0]
    n = lax.axis_size("grid")
    slabs = planes * rows
    chunk = local_orbs // n
    wc = w // NCH
    orb_r = orbitals.reshape(local_orbs, slabs, nx).transpose(1, 0, 2)
    adj_r = rotated_adj.reshape(w, slabs, nx).transpose(1, 0, 2)
    tiles = tile_map.shape[0]
    stored = jnp.take(
        rotation.reshape(tiles, norb // tiles, norb), tile_map, axis=0, mode="clip"
    ).reshape(norb, norb)
    vmem = pl.BlockSpec(memory_space=pltpu.VMEM)
    dma = pltpu.SemaphoreType.DMA
    result = pl.pallas_call(
        functools.partial(fields_kernel, n, planes, rows),
        out_shape=jax.ShapeDtypeStruct((slabs, local_orbs, nx), BF16),
        in_specs=[vmem] * 7,
        out_specs=vmem,
        scratch_shapes=[
            pltpu.VMEM((slabs, 3 * w, nx), BF16),
            pltpu.VMEM((local_orbs, 3 * w), BF16),
            pltpu.VMEM((slabs // 2, local_orbs, 2 * nx), F32),
            pltpu.VMEM((n, chunk, w), F32),
            pltpu.VMEM((n, chunk, w), F32),
            pltpu.VMEM((2 * n, chunk, w), F32),
            pltpu.VMEM((2, n, w // n, local_orbs), F32),
            pltpu.VMEM((2 * NCH, slabs, wc, nx), BF16),
            pltpu.VMEM((2 * NCH, slabs, wc, nx), BF16),
            pltpu.VMEM((2 * NCH, rows + 4, planes, wc, nx), BF16),
            dma((n,)), dma((n,)), dma((2 * n,)), dma((2 * n,)), dma((n,)), dma((n,)),
            dma((2 * NCH,)), dma((2 * NCH,)), dma((2 * NCH,)),
            dma((2 * NCH,)), dma((2 * NCH,)), dma((2 * NCH,)),
        ],
        compiler_params=pltpu.CompilerParams(
            collective_id=0, has_side_effects=True, vmem_limit_bytes=56 * 1024 * 1024
        ),
    )(
        orb_r, adj_r, stored, gap_inverse, level_adj.reshape(1, w),
        window_cols.reshape(1, w), potential.reshape(slabs, nx),
    )
    return result.transpose(1, 0, 2).reshape(orbitals.shape)


def solution(mesh):
    in_specs = (
        P("orb", None, "grid", None),
        P(None, None, "grid", None),
        P(),
        P(),
        P("orb", None),
        P(None, "grid", None),
        P(),
        P(),
    )
    out_specs = P("orb", None, "grid", None)
    return jax.shard_map(local, mesh=mesh, in_specs=in_specs, out_specs=out_specs, check_vma=False)
```

```python
import functools

import jax
import jax.numpy as jnp
from jax import lax
from jax.experimental import pallas as pl
from jax.experimental.pallas import tpu as pltpu
from jax.sharding import PartitionSpec as P

MESH = pl.DeviceIdType.MESH
NCH = 4
EARLY = 1
F32 = jnp.float32
BF16 = jnp.bfloat16
NT = (((1,), (1,)), ((), ()))
NN = (((1,), (0,)), ((), ()))


def dot(a, b, dims):
    return lax.dot_general(a, b, dims, preferred_element_type=F32)


def loop(count, by, step):
    def body(k, _):
        for u in range(by):
            step(k * by + u)
        return 0

    lax.fori_loop(0, count // by, body, 0)


def split3(x):
    hi = x.astype(BF16)
    rest = x - hi.astype(F32)
    mid = rest.astype(BF16)
    low = (rest - mid.astype(F32)).astype(BF16)
    return hi, mid, low


def fields_kernel(
    n, planes, rows,
    orb_ref, adj_ref, stored_ref, gap_ref, level_ref, cols_ref, pot_ref,
    app_ref, fac_ref,
    corr, rs_buf, ag_buf, gap_all, part, peer, wide,
    rs_send, rs_recv, ag_send, ag_recv, gap_send, gap_recv,
    sum_send, sum_recv, up_send, up_recv, down_send, down_recv,
):
    slabs, local_orbs, nx = orb_ref.shape
    w = adj_ref.shape[1]
    norb = stored_ref.shape[0]
    wc = w // NCH
    g = lax.axis_index("grid")
    o = lax.axis_index("orb")
    me = o * n + g
    other = 1 - o
    after = lax.rem(g + 1, n)
    before = lax.rem(g + n - 1, n)

    barrier = pltpu.get_barrier_semaphore()

    def greet(k, _):
        pl.semaphore_signal(
            barrier, inc=1, device_id=(lax.rem(g + k, n), o), device_id_type=MESH
        )
        return 0

    pl.semaphore_signal(barrier, inc=1, device_id=(g, other), device_id_type=MESH)
    lax.fori_loop(1, n, greet, 0)

    def rs_copy(k):
        to = lax.rem(g + k, n)
        return pltpu.make_async_remote_copy(
            src_ref=corr.at[to], dst_ref=rs_buf.at[k],
            send_sem=rs_send.at[k], recv_sem=rs_recv.at[k],
            device_id=(to, o), device_id_type=MESH,
        )

    def rs_start(k, _):
        rs_copy(k).start()
        return 0

    def sum_copy(half, ch):
        i = half * NCH + ch
        return pltpu.make_async_remote_copy(
            src_ref=part.at[i], dst_ref=peer.at[i],
            send_sem=sum_send.at[i], recv_sem=sum_recv.at[i],
            device_id=(g, other), device_id_type=MESH,
        )

    def up_copy(half, ch):
        i = half * NCH + ch
        return pltpu.make_async_remote_copy(
            src_ref=wide.at[i, pl.ds(rows, 2)], dst_ref=wide.at[i, pl.ds(0, 2)],
            send_sem=up_send.at[i], recv_sem=up_recv.at[i],
            device_id=(after, o), device_id_type=MESH,
        )

    def down_copy(half, ch):
        i = half * NCH + ch
        return pltpu.make_async_remote_copy(
            src_ref=wide.at[i, pl.ds(2, 2)], dst_ref=wide.at[i, pl.ds(rows + 2, 2)],
            send_sem=down_send.at[i], recv_sem=down_recv.at[i],
            device_id=(before, o), device_id_type=MESH,
        )

    def partials(half, factor_t):
        def step(k):
            pair = jnp.concatenate([orb_ref[2 * k], orb_ref[2 * k + 1]], axis=1)
            term = dot(factor_t, pair, NN).astype(BF16)
            for ch in range(NCH):
                fields = term[ch * wc : (ch + 1) * wc]
                part[half * NCH + ch, 2 * k] = fields[:, :nx]
                part[half * NCH + ch, 2 * k + 1] = fields[:, nx:]
            return 0

        loop(slabs // 2, 4, step)

    def column(row_ref):
        row = row_ref[...].astype(F32)
        return jnp.broadcast_to(row, (w, w)).T[:, :1]

    mine = pl.ds(pl.multiple_of(o * local_orbs, local_orbs), local_orbs)
    level_rows = lax.broadcasted_iota(jnp.int32, (w, norb), 1).astype(F32)
    hot = level_rows == column(cols_ref)
    hot16 = hot.astype(F32).astype(BF16)
    right_t = dot(hot16, stored_ref[mine, :], NT).astype(BF16)
    fac_ref[0] = right_t
    fac_ref[2] = right_t

    hi, mid, low = split3(gap_ref[...])
    gap_all[o] = dot(hot16, hi, NT) + dot(hot16, mid, NT) + dot(hot16, low, NT)
    gap_copy = pltpu.make_async_remote_copy(
        src_ref=gap_all.at[o], dst_ref=gap_all.at[o],
        send_sem=gap_send, recv_sem=gap_recv,
        device_id=(g, other), device_id_type=MESH,
    )
    pl.semaphore_wait(barrier, n)
    gap_copy.start()
    partials(0, right_t)
    for ch in range(EARLY):
        sum_copy(0, ch).start()

    corr[...] = jnp.zeros_like(corr)

    def corr_step(k):
        orbs = jnp.concatenate([orb_ref[4 * k + i] for i in range(4)], axis=1)
        adjs = jnp.concatenate([adj_ref[4 * k + i] for i in range(4)], axis=1)
        corr[...] += dot(orbs, adjs, NT).reshape(corr.shape)
        return 0

    loop(slabs // 4, 2, corr_step)
    lax.fori_loop(1, n, rs_start, 0)

    def stack_step(r):
        app_ref[r, :w] = adj_ref[r]
        return 0

    loop(slabs, 4, stack_step)

    ag_buf[me] = corr[g]

    def rs_take(k, _):
        rs_copy(k).wait_recv()
        ag_buf[me] += rs_buf[k]
        return 0

    lax.fori_loop(1, n, rs_take, 0)

    theirs = other * n + g
    cross_copy = pltpu.make_async_remote_copy(
        src_ref=ag_buf.at[me], dst_ref=ag_buf.at[me],
        send_sem=ag_send.at[0], recv_sem=ag_recv.at[0],
        device_id=(g, other), device_id_type=MESH,
    )

    def ag_copy(k, slot, first):
        return pltpu.make_async_remote_copy(
            src_ref=ag_buf.at[slot], dst_ref=ag_buf.at[slot],
            send_sem=ag_send.at[first + k], recv_sem=ag_recv.at[first + k],
            device_id=(lax.rem(g + k, n), o), device_id_type=MESH,
        )

    def ag_start(k, _):
        ag_copy(k, me, 0).start()
        return 0

    def ag_forward(k, _):
        ag_copy(k, theirs, n).start()
        return 0

    def ag_take(k, _):
        ag_copy(k, me, 0).wait_recv()
        ag_copy(k, theirs, n).wait_recv()
        return 0

    cross_copy.start()
    lax.fori_loop(1, n, ag_start, 0)
    for ch in range(EARLY, NCH):
        sum_copy(0, ch).start()
    cross_copy.wait_recv()
    lax.fori_loop(1, n, ag_forward, 0)
    lax.fori_loop(1, n, ag_take, 0)
    gap_copy.wait_recv()

    corr_t = ag_buf[...].reshape(norb, w).T
    parts_t = jnp.concatenate(split3(corr_t), axis=0)
    rotated = dot(parts_t, stored_ref[...], NN)
    coupling_in = rotated[:w] + rotated[w : 2 * w] + rotated[2 * w :]
    gap_cols = jnp.concatenate([gap_all[0], gap_all[1]], axis=1)
    coupling = gap_cols * coupling_in + jnp.where(hot, column(level_ref), 0.0)
    mixed = dot(jnp.concatenate(split3(coupling), axis=0), stored_ref[mine, :], NT)
    left_t = (mixed[:w] + mixed[w : 2 * w] + mixed[2 * w :]).astype(BF16)
    fac_ref[1] = left_t
    partials(1, left_t)
    for ch in range(NCH):
        sum_copy(1, ch).start()

    def combine(half, ch):
        i = half * NCH + ch
        sum_copy(half, ch).wait_recv()

        def step(p):
            for y in range(rows):
                r = p * rows + y
                wide[i, 2 + y, p] = (
                    part[i, r].astype(F32) + peer[i, r].astype(F32)
                ).astype(BF16)
            return 0

        loop(planes, 4, step)
        up_copy(half, ch).start()
        down_copy(half, ch).start()

    def stencil(half, ch):
        i = half * NCH + ch
        up_copy(half, ch).wait_recv()
        down_copy(half, ch).wait_recv()
        first = (half + 1) * w + ch * wc

        def step(p):
            lines = [wide[i, y, p].astype(F32) for y in range(rows + 4)]
            near_planes = [lax.rem(p + d, planes) for d in (1, planes - 1)]
            far_planes = [lax.rem(p + d, planes) for d in (2, planes - 2)]
            for y in range(rows):
                f = lines[y + 2]
                near = lines[y + 1] + lines[y + 3]
                far = lines[y] + lines[y + 4]
                for q in near_planes:
                    near = near + wide[i, 2 + y, q].astype(F32)
                for q in far_planes:
                    far = far + wide[i, 2 + y, q].astype(F32)
                near = near + pltpu.roll(f, 1, 1) + pltpu.roll(f, nx - 1, 1)
                far = far + pltpu.roll(f, 2, 1) + pltpu.roll(f, nx - 2, 1)
                r = p * rows + y
                diag = 3.75 + pot_ref[pl.ds(r, 1), :]
                value = diag * f - (2.0 / 3.0) * near + (1.0 / 24.0) * far
                app_ref[r, first : first + wc] = value.astype(BF16)
            return 0

        loop(planes, 4, step)

    for half in range(2):
        for ch in range(NCH):
            combine(half, ch)
            if ch:
                stencil(half, ch - 1)
        stencil(half, NCH - 1)

    def rs_done(k, _):
        rs_copy(k).wait_send()
        return 0

    def ag_done(k, _):
        ag_copy(k, me, 0).wait_send()
        ag_copy(k, theirs, n).wait_send()
        return 0

    lax.fori_loop(1, n, rs_done, 0)
    lax.fori_loop(1, n, ag_done, 0)
    cross_copy.wait_send()
    gap_copy.wait_send()
    for half in range(2):
        for ch in range(NCH):
            sum_copy(half, ch).wait_send()
            up_copy(half, ch).wait_send()
            down_copy(half, ch).wait_send()


def local(
    orbitals, rotated_adj, level_adj, rotation, gap_inverse, potential, window_cols, tile_map
):
    local_orbs, planes, rows, nx = orbitals.shape
    w = rotated_adj.shape[0]
    norb = rotation.shape[0]
    n = lax.axis_size("grid")
    slabs = planes * rows
    chunk = local_orbs // n
    wc = w // NCH
    orb_r = orbitals.reshape(local_orbs, slabs, nx).transpose(1, 0, 2)
    adj_r = rotated_adj.reshape(w, slabs, nx).transpose(1, 0, 2)
    tiles = tile_map.shape[0]
    stored = jnp.take(
        rotation.reshape(tiles, norb // tiles, norb), tile_map, axis=0, mode="clip"
    ).reshape(norb, norb)
    vmem = pl.BlockSpec(memory_space=pltpu.VMEM)
    dma = pltpu.SemaphoreType.DMA
    stacked, factors = pl.pallas_call(
        functools.partial(fields_kernel, n, planes, rows),
        out_shape=(
            jax.ShapeDtypeStruct((slabs, 3 * w, nx), BF16),
            jax.ShapeDtypeStruct((3, w, local_orbs), BF16),
        ),
        in_specs=[vmem] * 7,
        out_specs=(vmem, vmem),
        scratch_shapes=[
            pltpu.VMEM((n, chunk, w), F32),
            pltpu.VMEM((n, chunk, w), F32),
            pltpu.VMEM((2 * n, chunk, w), F32),
            pltpu.VMEM((2, w, local_orbs), F32),
            pltpu.VMEM((2 * NCH, slabs, wc, nx), BF16),
            pltpu.VMEM((2 * NCH, slabs, wc, nx), BF16),
            pltpu.VMEM((2 * NCH, rows + 4, planes, wc, nx), BF16),
            dma((n,)), dma((n,)), dma((2 * n,)), dma((2 * n,)), dma, dma,
            dma((2 * NCH,)), dma((2 * NCH,)), dma((2 * NCH,)),
            dma((2 * NCH,)), dma((2 * NCH,)), dma((2 * NCH,)),
        ],
        compiler_params=pltpu.CompilerParams(
            collective_id=0, has_side_effects=True, vmem_limit_bytes=56 * 1024 * 1024
        ),
    )(
        orb_r, adj_r, stored, gap_inverse, level_adj.reshape(1, w),
        window_cols.reshape(1, w), potential.reshape(slabs, nx),
    )
    mix_t = factors.reshape(3 * w, local_orbs)
    result = lax.dot_general(
        mix_t, stacked, (((0,), (1,)), ((), ())), preferred_element_type=F32
    ).astype(BF16)
    return result.reshape(orbitals.shape)


def solution(mesh):
    in_specs = (
        P("orb", None, "grid", None),
        P(None, None, "grid", None),
        P(),
        P(),
        P("orb", None),
        P(None, "grid", None),
        P(),
        P(),
    )
    out_specs = P("orb", None, "grid", None)
    return jax.shard_map(local, mesh=mesh, in_specs=in_specs, out_specs=out_specs, check_vma=False)
```

```python
import functools

import jax
import jax.numpy as jnp
from jax import lax
from jax.experimental import pallas as pl
from jax.experimental.pallas import tpu as pltpu
from jax.sharding import PartitionSpec as P

MESH = pl.DeviceIdType.MESH
NCH = 4
EARLY = 1
F32 = jnp.float32
BF16 = jnp.bfloat16
NT = (((1,), (1,)), ((), ()))
NN = (((1,), (0,)), ((), ()))


def dot(a, b, dims):
    return lax.dot_general(a, b, dims, preferred_element_type=F32)


def loop(count, by, step):
    def body(k, _):
        for u in range(by):
            step(k * by + u)
        return 0

    lax.fori_loop(0, count // by, body, 0)


def split3(x):
    hi = x.astype(BF16)
    rest = x - hi.astype(F32)
    mid = rest.astype(BF16)
    low = (rest - mid.astype(F32)).astype(BF16)
    return hi, mid, low


def fields_kernel(
    n, planes, rows,
    orb_ref, adj_ref, stored_ref, gap_ref, level_ref, cols_ref, pot_ref,
    app_ref, fac_ref,
    corr, rs_buf, ag_buf, gap_all, part, peer, wide,
    rs_send, rs_recv, ag_send, ag_recv, gap_send, gap_recv,
    sum_send, sum_recv, up_send, up_recv, down_send, down_recv,
):
    slabs, local_orbs, nx = orb_ref.shape
    w = adj_ref.shape[1]
    norb = stored_ref.shape[0]
    wc = w // NCH
    g = lax.axis_index("grid")
    o = lax.axis_index("orb")
    me = o * n + g
    other = 1 - o
    after = lax.rem(g + 1, n)
    before = lax.rem(g + n - 1, n)

    barrier = pltpu.get_barrier_semaphore()

    def greet(k, _):
        pl.semaphore_signal(
            barrier, inc=1, device_id=(lax.rem(g + k, n), o), device_id_type=MESH
        )
        return 0

    pl.semaphore_signal(barrier, inc=1, device_id=(g, other), device_id_type=MESH)
    lax.fori_loop(1, n, greet, 0)

    def rs_copy(k):
        to = lax.rem(g + k, n)
        return pltpu.make_async_remote_copy(
            src_ref=corr.at[to], dst_ref=rs_buf.at[k],
            send_sem=rs_send.at[k], recv_sem=rs_recv.at[k],
            device_id=(to, o), device_id_type=MESH,
        )

    def rs_start(k, _):
        rs_copy(k).start()
        return 0

    corr[...] = jnp.zeros_like(corr)

    def corr_step(k):
        orbs = jnp.concatenate([orb_ref[4 * k + i] for i in range(4)], axis=1)
        adjs = jnp.concatenate([adj_ref[4 * k + i] for i in range(4)], axis=1)
        corr[...] += dot(orbs, adjs, NT).reshape(corr.shape)
        return 0

    loop(slabs // 4, 2, corr_step)
    pl.semaphore_wait(barrier, n)
    lax.fori_loop(1, n, rs_start, 0)

    def sum_copy(half, ch):
        i = half * NCH + ch
        return pltpu.make_async_remote_copy(
            src_ref=part.at[i], dst_ref=peer.at[i],
            send_sem=sum_send.at[i], recv_sem=sum_recv.at[i],
            device_id=(g, other), device_id_type=MESH,
        )

    def up_copy(half, ch):
        i = half * NCH + ch
        return pltpu.make_async_remote_copy(
            src_ref=wide.at[i, pl.ds(rows, 2)], dst_ref=wide.at[i, pl.ds(0, 2)],
            send_sem=up_send.at[i], recv_sem=up_recv.at[i],
            device_id=(after, o), device_id_type=MESH,
        )

    def down_copy(half, ch):
        i = half * NCH + ch
        return pltpu.make_async_remote_copy(
            src_ref=wide.at[i, pl.ds(2, 2)], dst_ref=wide.at[i, pl.ds(rows + 2, 2)],
            send_sem=down_send.at[i], recv_sem=down_recv.at[i],
            device_id=(before, o), device_id_type=MESH,
        )

    def partials(half, factor_t):
        def step(k):
            pair = jnp.concatenate([orb_ref[2 * k], orb_ref[2 * k + 1]], axis=1)
            term = dot(factor_t, pair, NN).astype(BF16)
            for ch in range(NCH):
                fields = term[ch * wc : (ch + 1) * wc]
                part[half * NCH + ch, 2 * k] = fields[:, :nx]
                part[half * NCH + ch, 2 * k + 1] = fields[:, nx:]
            return 0

        loop(slabs // 2, 4, step)

    def column(row_ref):
        row = row_ref[...].astype(F32)
        return jnp.broadcast_to(row, (w, w)).T[:, :1]

    mine = pl.ds(pl.multiple_of(o * local_orbs, local_orbs), local_orbs)
    level_rows = lax.broadcasted_iota(jnp.int32, (w, norb), 1).astype(F32)
    hot = level_rows == column(cols_ref)
    hot16 = hot.astype(F32).astype(BF16)
    right_t = dot(hot16, stored_ref[mine, :], NT).astype(BF16)
    fac_ref[0] = right_t
    fac_ref[2] = right_t

    partials(0, right_t)
    for ch in range(EARLY):
        sum_copy(0, ch).start()

    hi, mid, low = split3(gap_ref[...])
    mine_gap = dot(hot16, hi, NT) + dot(hot16, mid, NT) + dot(hot16, low, NT)
    gap_all[o] = mine_gap.reshape(n, w // n, local_orbs)
    gap_cross = pltpu.make_async_remote_copy(
        src_ref=gap_all.at[o, g], dst_ref=gap_all.at[o, g],
        send_sem=gap_send.at[0], recv_sem=gap_recv.at[0],
        device_id=(g, other), device_id_type=MESH,
    )

    def gap_copy(k):
        return pltpu.make_async_remote_copy(
            src_ref=gap_all.at[other, g], dst_ref=gap_all.at[other, g],
            send_sem=gap_send.at[k], recv_sem=gap_recv.at[k],
            device_id=(lax.rem(g + k, n), o), device_id_type=MESH,
        )

    def gap_start(k, _):
        gap_copy(k).start()
        return 0

    gap_cross.start()

    ag_buf[me] = corr[g]

    def rs_take(k, _):
        rs_copy(k).wait_recv()
        ag_buf[me] += rs_buf[k]
        return 0

    lax.fori_loop(1, n, rs_take, 0)

    theirs = other * n + g
    cross_copy = pltpu.make_async_remote_copy(
        src_ref=ag_buf.at[me], dst_ref=ag_buf.at[me],
        send_sem=ag_send.at[0], recv_sem=ag_recv.at[0],
        device_id=(g, other), device_id_type=MESH,
    )

    def ag_copy(k, slot, first):
        return pltpu.make_async_remote_copy(
            src_ref=ag_buf.at[slot], dst_ref=ag_buf.at[slot],
            send_sem=ag_send.at[first + k], recv_sem=ag_recv.at[first + k],
            device_id=(lax.rem(g + k, n), o), device_id_type=MESH,
        )

    def ag_start(k, _):
        ag_copy(k, me, 0).start()
        return 0

    def ag_forward(k, _):
        ag_copy(k, theirs, n).start()
        return 0

    def ag_take(k, _):
        ag_copy(k, me, 0).wait_recv()
        ag_copy(k, theirs, n).wait_recv()
        gap_copy(k).wait_recv()
        return 0

    cross_copy.start()
    lax.fori_loop(1, n, ag_start, 0)
    for ch in range(EARLY, NCH):
        sum_copy(0, ch).start()
    cross_copy.wait_recv()
    lax.fori_loop(1, n, ag_forward, 0)
    gap_cross.wait_recv()
    lax.fori_loop(1, n, gap_start, 0)
    lax.fori_loop(1, n, ag_take, 0)

    corr_t = ag_buf[...].reshape(norb, w).T
    parts_t = jnp.concatenate(split3(corr_t), axis=0)
    rotated = dot(parts_t, stored_ref[...], NN)
    coupling_in = rotated[:w] + rotated[w : 2 * w] + rotated[2 * w :]
    gap_cols = jnp.concatenate([gap_all[i].reshape(w, local_orbs) for i in range(2)], axis=1)
    coupling = gap_cols * coupling_in + jnp.where(hot, column(level_ref), 0.0)
    mixed = dot(jnp.concatenate(split3(coupling), axis=0), stored_ref[mine, :], NT)
    left_t = (mixed[:w] + mixed[w : 2 * w] + mixed[2 * w :]).astype(BF16)
    fac_ref[1] = left_t
    partials(1, left_t)
    for ch in range(NCH):
        sum_copy(1, ch).start()

    def stack_step(r):
        app_ref[r, :w] = adj_ref[r]
        return 0

    loop(slabs, 4, stack_step)

    def combine(half, ch):
        i = half * NCH + ch
        sum_copy(half, ch).wait_recv()

        def step(p):
            for y in range(rows):
                r = p * rows + y
                wide[i, 2 + y, p] = (
                    part[i, r].astype(F32) + peer[i, r].astype(F32)
                ).astype(BF16)
            return 0

        loop(planes, 4, step)
        up_copy(half, ch).start()
        down_copy(half, ch).start()

    def stencil(half, ch):
        i = half * NCH + ch
        up_copy(half, ch).wait_recv()
        down_copy(half, ch).wait_recv()
        first = (half + 1) * w + ch * wc

        def step(p):
            lines = [wide[i, y, p].astype(F32) for y in range(rows + 4)]
            near_planes = [lax.rem(p + d, planes) for d in (1, planes - 1)]
            far_planes = [lax.rem(p + d, planes) for d in (2, planes - 2)]
            for y in range(rows):
                f = lines[y + 2]
                near = lines[y + 1] + lines[y + 3]
                far = lines[y] + lines[y + 4]
                for q in near_planes:
                    near = near + wide[i, 2 + y, q].astype(F32)
                for q in far_planes:
                    far = far + wide[i, 2 + y, q].astype(F32)
                near = near + pltpu.roll(f, 1, 1) + pltpu.roll(f, nx - 1, 1)
                far = far + pltpu.roll(f, 2, 1) + pltpu.roll(f, nx - 2, 1)
                r = p * rows + y
                diag = 3.75 + pot_ref[pl.ds(r, 1), :]
                value = diag * f - (2.0 / 3.0) * near + (1.0 / 24.0) * far
                app_ref[r, first : first + wc] = value.astype(BF16)
            return 0

        loop(planes, 4, step)

    for half in range(2):
        for ch in range(NCH):
            combine(half, ch)
            if ch:
                stencil(half, ch - 1)
        stencil(half, NCH - 1)

    def rs_done(k, _):
        rs_copy(k).wait_send()
        return 0

    def ag_done(k, _):
        ag_copy(k, me, 0).wait_send()
        ag_copy(k, theirs, n).wait_send()
        gap_copy(k).wait_send()
        return 0

    lax.fori_loop(1, n, rs_done, 0)
    lax.fori_loop(1, n, ag_done, 0)
    cross_copy.wait_send()
    gap_cross.wait_send()
    for half in range(2):
        for ch in range(NCH):
            sum_copy(half, ch).wait_send()
            up_copy(half, ch).wait_send()
            down_copy(half, ch).wait_send()


def local(
    orbitals, rotated_adj, level_adj, rotation, gap_inverse, potential, window_cols, tile_map
):
    local_orbs, planes, rows, nx = orbitals.shape
    w = rotated_adj.shape[0]
    norb = rotation.shape[0]
    n = lax.axis_size("grid")
    slabs = planes * rows
    chunk = local_orbs // n
    wc = w // NCH
    orb_r = orbitals.reshape(local_orbs, slabs, nx).transpose(1, 0, 2)
    adj_r = rotated_adj.reshape(w, slabs, nx).transpose(1, 0, 2)
    tiles = tile_map.shape[0]
    stored = jnp.take(
        rotation.reshape(tiles, norb // tiles, norb), tile_map, axis=0, mode="clip"
    ).reshape(norb, norb)
    vmem = pl.BlockSpec(memory_space=pltpu.VMEM)
    dma = pltpu.SemaphoreType.DMA
    stacked, factors = pl.pallas_call(
        functools.partial(fields_kernel, n, planes, rows),
        out_shape=(
            jax.ShapeDtypeStruct((slabs, 3 * w, nx), BF16),
            jax.ShapeDtypeStruct((3, w, local_orbs), BF16),
        ),
        in_specs=[vmem] * 7,
        out_specs=(vmem, vmem),
        scratch_shapes=[
            pltpu.VMEM((n, chunk, w), F32),
            pltpu.VMEM((n, chunk, w), F32),
            pltpu.VMEM((2 * n, chunk, w), F32),
            pltpu.VMEM((2, n, w // n, local_orbs), F32),
            pltpu.VMEM((2 * NCH, slabs, wc, nx), BF16),
            pltpu.VMEM((2 * NCH, slabs, wc, nx), BF16),
            pltpu.VMEM((2 * NCH, rows + 4, planes, wc, nx), BF16),
            dma((n,)), dma((n,)), dma((2 * n,)), dma((2 * n,)), dma((n,)), dma((n,)),
            dma((2 * NCH,)), dma((2 * NCH,)), dma((2 * NCH,)),
            dma((2 * NCH,)), dma((2 * NCH,)), dma((2 * NCH,)),
        ],
        compiler_params=pltpu.CompilerParams(
            collective_id=0, has_side_effects=True, vmem_limit_bytes=56 * 1024 * 1024
        ),
    )(
        orb_r, adj_r, stored, gap_inverse, level_adj.reshape(1, w),
        window_cols.reshape(1, w), potential.reshape(slabs, nx),
    )
    mix_t = factors.reshape(3 * w, local_orbs)
    result = lax.dot_general(
        mix_t, stacked, (((0,), (1,)), ((), ())), preferred_element_type=F32
    ).astype(BF16)
    return result.reshape(orbitals.shape)


def solution(mesh):
    in_specs = (
        P("orb", None, "grid", None),
        P(None, None, "grid", None),
        P(),
        P(),
        P("orb", None),
        P(None, "grid", None),
        P(),
        P(),
    )
    out_specs = P("orb", None, "grid", None)
    return jax.shard_map(local, mesh=mesh, in_specs=in_specs, out_specs=out_specs, check_vma=False)
```

```python
import functools

import jax
import jax.numpy as jnp
from jax import lax
from jax.experimental import pallas as pl
from jax.experimental.pallas import tpu as pltpu
from jax.sharding import PartitionSpec as P

MESH = pl.DeviceIdType.MESH
NCH = 4
EARLY = 1
F32 = jnp.float32
BF16 = jnp.bfloat16
NT = (((1,), (1,)), ((), ()))
NN = (((1,), (0,)), ((), ()))


def dot(a, b, dims):
    return lax.dot_general(a, b, dims, preferred_element_type=F32)


def loop(count, by, step):
    def body(k, _):
        for u in range(by):
            step(k * by + u)
        return 0

    lax.fori_loop(0, count // by, body, 0)


def split3(x):
    hi = x.astype(BF16)
    rest = x - hi.astype(F32)
    mid = rest.astype(BF16)
    low = (rest - mid.astype(F32)).astype(BF16)
    return hi, mid, low


def fields_kernel(
    n, planes, rows,
    orb_ref, adj_ref, stored_ref, gap_ref, level_ref, cols_ref, pot_ref,
    app_ref, fac_ref,
    corr, rs_buf, ag_buf, gap_all, part, peer, wide,
    rs_send, rs_recv, ag_send, ag_recv, gap_send, gap_recv,
    sum_send, sum_recv, up_send, up_recv, down_send, down_recv,
):
    slabs, local_orbs, nx = orb_ref.shape
    w = adj_ref.shape[1]
    norb = stored_ref.shape[0]
    wc = w // NCH
    g = lax.axis_index("grid")
    o = lax.axis_index("orb")
    me = o * n + g
    other = 1 - o
    after = lax.rem(g + 1, n)
    before = lax.rem(g + n - 1, n)

    barrier = pltpu.get_barrier_semaphore()

    def greet(k, _):
        pl.semaphore_signal(
            barrier, inc=1, device_id=(lax.rem(g + k, n), o), device_id_type=MESH
        )
        return 0

    pl.semaphore_signal(barrier, inc=1, device_id=(g, other), device_id_type=MESH)
    lax.fori_loop(1, n, greet, 0)

    def rs_copy(k):
        to = lax.rem(g + k, n)
        return pltpu.make_async_remote_copy(
            src_ref=corr.at[to], dst_ref=rs_buf.at[k],
            send_sem=rs_send.at[k], recv_sem=rs_recv.at[k],
            device_id=(to, o), device_id_type=MESH,
        )

    def rs_start(k, _):
        rs_copy(k).start()
        return 0

    corr[...] = jnp.zeros_like(corr)

    def corr_step(k):
        orbs = jnp.concatenate([orb_ref[4 * k + i] for i in range(4)], axis=1)
        adjs = jnp.concatenate([adj_ref[4 * k + i] for i in range(4)], axis=1)
        corr[...] += dot(orbs, adjs, NT).reshape(corr.shape)
        return 0

    loop(slabs // 4, 4, corr_step)
    pl.semaphore_wait(barrier, n)
    lax.fori_loop(1, n, rs_start, 0)

    def sum_copy(half, ch):
        i = half * NCH + ch
        return pltpu.make_async_remote_copy(
            src_ref=part.at[i], dst_ref=peer.at[i],
            send_sem=sum_send.at[i], recv_sem=sum_recv.at[i],
            device_id=(g, other), device_id_type=MESH,
        )

    def up_copy(half, ch):
        i = half * NCH + ch
        return pltpu.make_async_remote_copy(
            src_ref=wide.at[i, pl.ds(rows, 2)], dst_ref=wide.at[i, pl.ds(0, 2)],
            send_sem=up_send.at[i], recv_sem=up_recv.at[i],
            device_id=(after, o), device_id_type=MESH,
        )

    def down_copy(half, ch):
        i = half * NCH + ch
        return pltpu.make_async_remote_copy(
            src_ref=wide.at[i, pl.ds(2, 2)], dst_ref=wide.at[i, pl.ds(rows + 2, 2)],
            send_sem=down_send.at[i], recv_sem=down_recv.at[i],
            device_id=(before, o), device_id_type=MESH,
        )

    def partials(half, factor_t):
        def step(k):
            pair = jnp.concatenate([orb_ref[2 * k], orb_ref[2 * k + 1]], axis=1)
            term = dot(factor_t, pair, NN).astype(BF16)
            for ch in range(NCH):
                fields = term[ch * wc : (ch + 1) * wc]
                part[half * NCH + ch, 2 * k] = fields[:, :nx]
                part[half * NCH + ch, 2 * k + 1] = fields[:, nx:]
            return 0

        loop(slabs // 2, 8, step)

    def column(row_ref):
        row = row_ref[...].astype(F32)
        return jnp.broadcast_to(row, (w, w)).T[:, :1]

    mine = pl.ds(pl.multiple_of(o * local_orbs, local_orbs), local_orbs)
    level_rows = lax.broadcasted_iota(jnp.int32, (w, norb), 1).astype(F32)
    hot = level_rows == column(cols_ref)
    hot16 = hot.astype(F32).astype(BF16)
    right_t = dot(hot16, stored_ref[mine, :], NT).astype(BF16)
    fac_ref[0] = right_t
    fac_ref[2] = right_t

    partials(0, right_t)
    for ch in range(EARLY):
        sum_copy(0, ch).start()

    hi, mid, low = split3(gap_ref[...])
    mine_gap = dot(hot16, hi, NT) + dot(hot16, mid, NT) + dot(hot16, low, NT)
    gap_all[o] = mine_gap.reshape(n, w // n, local_orbs)
    gap_cross = pltpu.make_async_remote_copy(
        src_ref=gap_all.at[o, g], dst_ref=gap_all.at[o, g],
        send_sem=gap_send.at[0], recv_sem=gap_recv.at[0],
        device_id=(g, other), device_id_type=MESH,
    )

    def gap_copy(k):
        return pltpu.make_async_remote_copy(
            src_ref=gap_all.at[other, g], dst_ref=gap_all.at[other, g],
            send_sem=gap_send.at[k], recv_sem=gap_recv.at[k],
            device_id=(lax.rem(g + k, n), o), device_id_type=MESH,
        )

    def gap_start(k, _):
        gap_copy(k).start()
        return 0

    gap_cross.start()

    ag_buf[me] = corr[g]

    def rs_take(k, _):
        rs_copy(k).wait_recv()
        ag_buf[me] += rs_buf[k]
        return 0

    lax.fori_loop(1, n, rs_take, 0)

    theirs = other * n + g
    cross_copy = pltpu.make_async_remote_copy(
        src_ref=ag_buf.at[me], dst_ref=ag_buf.at[me],
        send_sem=ag_send.at[0], recv_sem=ag_recv.at[0],
        device_id=(g, other), device_id_type=MESH,
    )

    def ag_copy(k, slot, first):
        return pltpu.make_async_remote_copy(
            src_ref=ag_buf.at[slot], dst_ref=ag_buf.at[slot],
            send_sem=ag_send.at[first + k], recv_sem=ag_recv.at[first + k],
            device_id=(lax.rem(g + k, n), o), device_id_type=MESH,
        )

    def ag_start(k, _):
        ag_copy(k, me, 0).start()
        return 0

    def ag_forward(k, _):
        ag_copy(k, theirs, n).start()
        return 0

    def ag_take(k, _):
        ag_copy(k, me, 0).wait_recv()
        ag_copy(k, theirs, n).wait_recv()
        gap_copy(k).wait_recv()
        return 0

    cross_copy.start()
    lax.fori_loop(1, n, ag_start, 0)
    for ch in range(EARLY, NCH):
        sum_copy(0, ch).start()
    cross_copy.wait_recv()
    lax.fori_loop(1, n, ag_forward, 0)
    gap_cross.wait_recv()
    lax.fori_loop(1, n, gap_start, 0)
    lax.fori_loop(1, n, ag_take, 0)

    corr_t = ag_buf[...].reshape(norb, w).T
    parts_t = jnp.concatenate(split3(corr_t), axis=0)
    rotated = dot(parts_t, stored_ref[...], NN)
    coupling_in = rotated[:w] + rotated[w : 2 * w] + rotated[2 * w :]
    gap_cols = jnp.concatenate([gap_all[i].reshape(w, local_orbs) for i in range(2)], axis=1)
    coupling = gap_cols * coupling_in + jnp.where(hot, column(level_ref), 0.0)
    mixed = dot(jnp.concatenate(split3(coupling), axis=0), stored_ref[mine, :], NT)
    left_t = (mixed[:w] + mixed[w : 2 * w] + mixed[2 * w :]).astype(BF16)
    fac_ref[1] = left_t
    partials(1, left_t)
    for ch in range(NCH):
        sum_copy(1, ch).start()

    def stack_step(r):
        app_ref[r, :w] = adj_ref[r]
        return 0

    loop(slabs, 4, stack_step)

    def combine(half, ch):
        i = half * NCH + ch
        sum_copy(half, ch).wait_recv()

        def step(p):
            for y in range(rows):
                r = p * rows + y
                wide[i, 2 + y, p] = (
                    part[i, r].astype(F32) + peer[i, r].astype(F32)
                ).astype(BF16)
            return 0

        loop(planes, planes, step)
        up_copy(half, ch).start()
        down_copy(half, ch).start()

    def stencil(half, ch):
        i = half * NCH + ch
        up_copy(half, ch).wait_recv()
        down_copy(half, ch).wait_recv()
        first = (half + 1) * w + ch * wc

        def step(p):
            lines = [wide[i, y, p].astype(F32) for y in range(rows + 4)]
            near_planes = [lax.rem(p + d, planes) for d in (1, planes - 1)]
            far_planes = [lax.rem(p + d, planes) for d in (2, planes - 2)]
            for y in range(rows):
                f = lines[y + 2]
                near = lines[y + 1] + lines[y + 3]
                far = lines[y] + lines[y + 4]
                for q in near_planes:
                    near = near + wide[i, 2 + y, q].astype(F32)
                for q in far_planes:
                    far = far + wide[i, 2 + y, q].astype(F32)
                near = near + pltpu.roll(f, 1, 1) + pltpu.roll(f, nx - 1, 1)
                far = far + pltpu.roll(f, 2, 1) + pltpu.roll(f, nx - 2, 1)
                r = p * rows + y
                diag = 3.75 + pot_ref[pl.ds(r, 1), :]
                value = diag * f - (2.0 / 3.0) * near + (1.0 / 24.0) * far
                app_ref[r, first : first + wc] = value.astype(BF16)
            return 0

        loop(planes, planes, step)

    for half in range(2):
        for ch in range(NCH):
            combine(half, ch)
            if ch:
                stencil(half, ch - 1)
        stencil(half, NCH - 1)

    def rs_done(k, _):
        rs_copy(k).wait_send()
        return 0

    def ag_done(k, _):
        ag_copy(k, me, 0).wait_send()
        ag_copy(k, theirs, n).wait_send()
        gap_copy(k).wait_send()
        return 0

    lax.fori_loop(1, n, rs_done, 0)
    lax.fori_loop(1, n, ag_done, 0)
    cross_copy.wait_send()
    gap_cross.wait_send()
    for half in range(2):
        for ch in range(NCH):
            sum_copy(half, ch).wait_send()
            up_copy(half, ch).wait_send()
            down_copy(half, ch).wait_send()


def local(
    orbitals, rotated_adj, level_adj, rotation, gap_inverse, potential, window_cols, tile_map
):
    local_orbs, planes, rows, nx = orbitals.shape
    w = rotated_adj.shape[0]
    norb = rotation.shape[0]
    n = lax.axis_size("grid")
    slabs = planes * rows
    chunk = local_orbs // n
    wc = w // NCH
    orb_r = orbitals.reshape(local_orbs, slabs, nx).transpose(1, 0, 2)
    adj_r = rotated_adj.reshape(w, slabs, nx).transpose(1, 0, 2)
    tiles = tile_map.shape[0]
    stored = jnp.take(
        rotation.reshape(tiles, norb // tiles, norb), tile_map, axis=0, mode="clip"
    ).reshape(norb, norb)
    vmem = pl.BlockSpec(memory_space=pltpu.VMEM)
    dma = pltpu.SemaphoreType.DMA
    stacked, factors = pl.pallas_call(
        functools.partial(fields_kernel, n, planes, rows),
        out_shape=(
            jax.ShapeDtypeStruct((slabs, 3 * w, nx), BF16),
            jax.ShapeDtypeStruct((3, w, local_orbs), BF16),
        ),
        in_specs=[vmem] * 7,
        out_specs=(vmem, vmem),
        scratch_shapes=[
            pltpu.VMEM((n, chunk, w), F32),
            pltpu.VMEM((n, chunk, w), F32),
            pltpu.VMEM((2 * n, chunk, w), F32),
            pltpu.VMEM((2, n, w // n, local_orbs), F32),
            pltpu.VMEM((2 * NCH, slabs, wc, nx), BF16),
            pltpu.VMEM((2 * NCH, slabs, wc, nx), BF16),
            pltpu.VMEM((2 * NCH, rows + 4, planes, wc, nx), BF16),
            dma((n,)), dma((n,)), dma((2 * n,)), dma((2 * n,)), dma((n,)), dma((n,)),
            dma((2 * NCH,)), dma((2 * NCH,)), dma((2 * NCH,)),
            dma((2 * NCH,)), dma((2 * NCH,)), dma((2 * NCH,)),
        ],
        compiler_params=pltpu.CompilerParams(
            collective_id=0, has_side_effects=True, vmem_limit_bytes=56 * 1024 * 1024
        ),
    )(
        orb_r, adj_r, stored, gap_inverse, level_adj.reshape(1, w),
        window_cols.reshape(1, w), potential.reshape(slabs, nx),
    )
    mix_t = factors.reshape(3 * w, local_orbs)
    result = lax.dot_general(
        mix_t, stacked, (((0,), (1,)), ((), ())), preferred_element_type=F32
    ).astype(BF16)
    return result.reshape(orbitals.shape)


def solution(mesh):
    in_specs = (
        P("orb", None, "grid", None),
        P(None, None, "grid", None),
        P(),
        P(),
        P("orb", None),
        P(None, "grid", None),
        P(),
        P(),
    )
    out_specs = P("orb", None, "grid", None)
    return jax.shard_map(local, mesh=mesh, in_specs=in_specs, out_specs=out_specs, check_vma=False)
```
